32 devices in a mesh: gx: 4 (over y, core), gy: 8 (over z, x).
Axes of the slice: x: 2, y: 2, z: 4, core: 2. Of those that a mesh axis runs over, the one named last changes fastest.
Arguments:
- multipoles: bfloat16 [136, 2048], P(None, ('gx', 'gy')), may hold values from -6 to 6
- parent_ops: bfloat16 [4, 36992], replicated, may hold values from -0.1875 to 0.1875
- translators: bfloat16 [158, 36992], replicated, may hold values from -0.0390625 to 0.0390625
- fine_exports: int32 [32, 8, 32], P(('gx', 'gy')), may hold values from 0 to 63, as said below
- fine_sides: int32 [32, 2, 16], P(('gx', 'gy')), may hold values from 0 to 63, as said below
- fine_lists: int32 [189, 2048], P(None, ('gx', 'gy')), may hold values from 0 to 351
- fine_flags: int32 [189, 2048], P(None, ('gx', 'gy')), may hold values 0 or 1
- coarse_exports: int32 [32, 8, 4], P(('gx', 'gy')), may hold values from 0 to 7, as said below
- coarse_sides: int32 [32, 2, 2], P(('gx', 'gy')), may hold values from 0 to 7, as said below
- coarse_lists: int32 [189, 256], P(None, ('gx', 'gy')), may hold values from 0 to 43
- coarse_flags: int32 [189, 256], P(None, ('gx', 'gy')), may hold values 0 or 1
Outputs:
- fine_locals: float32 [136, 2048], P(None, ('gx', 'gy'))
- coarse_locals: float32 [136, 256], P(None, ('gx', 'gy'))
The draws below stay inside these ranges and needn't reach their ends.
Inputs may be any that keep to these rules, and one draw needn't show every extreme that they name: `fine_sides`: entries of the exports and sides are cells of the sending device, distinct within each row; the first row of sides goes to the next gx row, the second to the previous one. `fine_exports`: entries are cells of the sending device, distinct within each row. `coarse_exports`: entries are coarse cells of the sending device, distinct within each row. `coarse_sides`: entries are coarse cells of the sending device, distinct within each row. `fine_lists`: A list entry names a place in the owning device's fine source buffer. `coarse_lists`: A list entry names a place in the owning device's coarse source buffer.
All inputs are finite; a program needn't handle non-finite values. No bound on the sum of `fine_flags` or of `coarse_flags` on one device may be relied on, other than what follows from the above.
Results may differ from the reference program's by a relative error of at most 0.0029.
Values may be sent and summed in bfloat16 or wider, within the bound.
A program may use at most 128 MiB of HBM per device.

```python
import jax
import jax.numpy as jnp
import numpy as np
from jax import lax

K = 136
LIST = 189
DIRS = 316
CF = 64
CP = 8
CAP = 32
SIDE = 16
CAPC = 4
SIDEC = 2
BUF = 352
BUFC = 44
NF = 2048
NC = 256
N_GX = 4
N_GY = 8
DEVICES = 32


def distinct_rows(key, rows, pool, count):
    keys = jax.random.split(key, rows)
    picks = jax.vmap(lambda one_key: jax.random.permutation(one_key, pool)[:count])(keys)
    return picks.astype(jnp.int32)


def draw_fine_exports(key, part):
    key = jax.random.fold_in(key, 11)
    return distinct_rows(key, DEVICES * N_GY, CF, CAP).reshape(DEVICES, N_GY, CAP)


def draw_fine_sides(key, part):
    key = jax.random.fold_in(key, 12)
    return distinct_rows(key, DEVICES * 2, CF, SIDE).reshape(DEVICES, 2, SIDE)


def draw_coarse_exports(key, part):
    key = jax.random.fold_in(key, 13)
    return distinct_rows(key, DEVICES * N_GY, CP, CAPC).reshape(DEVICES, N_GY, CAPC)


def draw_coarse_sides(key, part):
    key = jax.random.fold_in(key, 14)
    return distinct_rows(key, DEVICES * 2, CP, SIDEC).reshape(DEVICES, 2, SIDEC)


def with_ends(values, own_key, low, largest):
    index_at = [jax.random.randint(jax.random.fold_in(own_key, axis), (), 0, length) for axis, length in enumerate(values.shape)]
    widest = values.shape.index(max(values.shape))
    beside = index_at[:widest] + [(index_at[widest] + 1) % values.shape[widest]] + index_at[widest + 1:]
    return values.at[tuple(index_at)].set(low).at[tuple(beside)].set(largest)


def block_levels(own_key, dims, cuts, least, top_value):
    def one(position, parts):
        draws = jax.random.uniform(jax.random.fold_in(jax.random.fold_in(own_key, 6), position), (parts,), jnp.float32, least / len(cuts), top_value / len(cuts))
        return jnp.repeat(jnp.exp(draws), dims[position] // parts).reshape((-1,) + (1,) * (len(dims) - position - 1))

    gain = one(*cuts[0])
    for cut in cuts[1:]:
        gain = gain * one(*cut)
    return gain


def centred(rng, shape, scale, bound, cuts=(), kind=jnp.bfloat16):
    entries = scale * jax.random.normal(rng, shape, jnp.float32)
    if cuts:
        entries = entries * block_levels(rng, shape, cuts, -0.22, 0.18)
    return jnp.clip(entries, -bound, bound).astype(kind)


def setup_inputs(seed: int = 0) -> dict:
    seeds = jax.random.split(jax.random.key(seed), 12)
    multipoles = centred(seeds[0], (K, NF), 1.0, 6.0, ((1, 32),))
    parent_ops = centred(seeds[1], (4, 2 * K * K), (8 * K) ** -0.5, 0.1875)
    translators = centred(seeds[2], (DIRS // 2, 2 * K * K), (K * LIST) ** -0.5, 0.0390625)
    fine_exports = draw_fine_exports(jax.random.fold_in(seeds[11], 71), 0)
    fine_sides = draw_fine_sides(jax.random.fold_in(seeds[11], 71), 0)
    fine_lists = with_ends(jax.random.randint(seeds[5], (LIST, NF), 0, BUF), jax.random.fold_in(seeds[5], 1), 0, BUF - 1).astype(jnp.int32)
    fine_flags = with_ends((jax.random.randint(seeds[6], (LIST, NF), 0, 8) < 7).astype(jnp.int32), jax.random.fold_in(seeds[6], 1), 0, 1)
    coarse_exports = draw_coarse_exports(jax.random.fold_in(seeds[11], 71), 0)
    coarse_sides = draw_coarse_sides(jax.random.fold_in(seeds[11], 71), 0)
    coarse_lists = with_ends(jax.random.randint(seeds[9], (LIST, NC), 0, BUFC), jax.random.fold_in(seeds[9], 1), 0, BUFC - 1).astype(jnp.int32)
    coarse_flags = with_ends((jax.random.randint(seeds[10], (LIST, NC), 0, 8) < 7).astype(jnp.int32), jax.random.fold_in(seeds[10], 1), 0, 1)
    return {"multipoles": multipoles, "parent_ops": parent_ops, "translators": translators, "fine_exports": fine_exports, "fine_sides": fine_sides, "fine_lists": fine_lists, "fine_flags": fine_flags, "coarse_exports": coarse_exports, "coarse_sides": coarse_sides, "coarse_lists": coarse_lists, "coarse_flags": coarse_flags}


def direction_table():
    far_offsets = {}
    for shift_x in range(-3, 4):
        for shift_y in range(-3, 4):
            for shift_z in range(-3, 4):
                if max(abs(shift_x), abs(shift_y), abs(shift_z)) > 1:
                    far_offsets[(shift_x, shift_y, shift_z)] = len(far_offsets)
    result = np.zeros((8, 189), np.int32)
    for octant in range(8):
        own_x, own_y, own_z = octant % 2, octant // 2 % 2, octant // 4
        column = 0
        for parent_x in (-1, 0, 1):
            for parent_y in (-1, 0, 1):
                for parent_z in (-1, 0, 1):
                    for child in range(8):
                        step_x = 2 * parent_x + child % 2 - own_x
                        step_y = 2 * parent_y + child // 2 % 2 - own_y
                        step_z = 2 * parent_z + child // 4 - own_z
                        if max(abs(step_x), abs(step_y), abs(step_z)) > 1:
                            result[octant, column] = far_offsets[(step_x, step_y, step_z)]
                            column = column + 1
    return result


def level_locals(mult, exports, sides, lists, flags, chosen):
    coeffs = mult.shape[0]
    cell_count = mult.shape[1] // (N_GX * N_GY)
    grid = mult.reshape(coeffs, N_GX, N_GY, cell_count)
    cap_row = exports.shape[2]
    side_cells = sides.shape[2]
    exp_grid = exports.reshape(N_GX, N_GY, N_GY, cap_row)
    side_grid = sides.reshape(N_GX, N_GY, 2, side_cells)
    peers = jnp.arange(N_GY, dtype=jnp.int32)

    def one_device(device):
        row_index = device // N_GY
        col_index = device % N_GY
        row_block = grid[:, row_index]
        wanted = exp_grid[row_index, :, col_index]
        from_row = row_block[:, peers[:, None], wanted]
        lower = jnp.maximum(row_index - 1, 0)
        upper = jnp.minimum(row_index + 1, N_GX - 1)
        below = grid[:, lower, col_index][:, side_grid[lower, col_index, 0]]
        above = grid[:, upper, col_index][:, side_grid[upper, col_index, 1]]
        below = jnp.where(row_index > 0, below, jnp.zeros_like(below))
        above = jnp.where(row_index < N_GX - 1, above, jnp.zeros_like(above))
        own = grid[:, row_index, col_index]
        buffer = jnp.concatenate([own, from_row.reshape(coeffs, -1), below, above], axis=1)
        start = (device * cell_count).astype(jnp.int32)
        picks = lax.dynamic_slice_in_dim(lists, start, cell_count, 1)
        live = lax.dynamic_slice_in_dim(flags, start, cell_count, 1)
        gathered = buffer[:, picks]
        gathered = jnp.where(live[None] > 0, gathered, jnp.zeros_like(gathered)).astype(jnp.float32)
        grouped = gathered.reshape(coeffs, picks.shape[0], cell_count // 8, 8)
        result = jnp.einsum("ojkl,ljqo->kqo", chosen, grouped, precision=lax.Precision.HIGHEST)
        return result.reshape(coeffs, cell_count)

    stacked = lax.map(one_device, jnp.arange(N_GX * N_GY, dtype=jnp.int32))
    return jnp.transpose(stacked, (1, 0, 2)).reshape(coeffs, -1)


def reference(multipoles, parent_ops, translators, fine_exports, fine_sides, fine_lists, fine_flags, coarse_exports, coarse_sides, coarse_lists, coarse_flags):
    coeffs = multipoles.shape[0]
    octant_ops = parent_ops.reshape(8, coeffs, coeffs)
    offset_ops = translators.reshape(-1, coeffs, coeffs)
    children = multipoles.astype(jnp.float32).reshape(coeffs, -1, 8)
    coarse = jnp.einsum("okl,lqo->kq", octant_ops.astype(jnp.float32), children, precision=lax.Precision.HIGHEST).astype(jnp.bfloat16)
    dir_table = jnp.asarray(direction_table())
    chosen = offset_ops[dir_table].astype(jnp.float32)
    fine_locals = level_locals(multipoles, fine_exports, fine_sides, fine_lists, fine_flags, chosen)
    coarse_locals = level_locals(coarse, coarse_exports, coarse_sides, coarse_lists, coarse_flags, chosen)
    return (fine_locals, coarse_locals)
```

```python
import functools

import jax
import jax.numpy as jnp
import ml_dtypes
import numpy as np
from jax import lax
from jax.experimental import pallas as pl
from jax.experimental.pallas import tpu as pltpu
from jax.sharding import PartitionSpec as P


def passed_along(block, axis, distance):
    devices = range(lax.axis_size(axis))
    route = [(i - distance, i) for i in devices if i - distance in devices]
    return lax.ppermute(block, axis, route)


def direction_table():
    far_offsets = {}
    for shift_x in range(-3, 4):
        for shift_y in range(-3, 4):
            for shift_z in range(-3, 4):
                if max(abs(shift_x), abs(shift_y), abs(shift_z)) > 1:
                    far_offsets[shift_x, shift_y, shift_z] = len(far_offsets)
    result = np.zeros((8, 189), np.int32)
    for octant in range(8):
        own_x, own_y, own_z = (octant % 2, octant // 2 % 2, octant // 4)
        column = 0
        for parent_x in (-1, 0, 1):
            for parent_y in (-1, 0, 1):
                for parent_z in (-1, 0, 1):
                    for child in range(8):
                        step_x = 2 * parent_x + child % 2 - own_x
                        step_y = 2 * parent_y + child // 2 % 2 - own_y
                        step_z = 2 * parent_z + child // 4 - own_z
                        if max(abs(step_x), abs(step_y), abs(step_z)) > 1:
                            result[octant, column] = far_offsets[step_x, step_y, step_z]
                            column = column + 1
    return result


def entry_to_lane():
    table = direction_table()
    result = np.zeros((8, 189, 512), np.float32)
    for octant in range(8):
        for entry in range(189):
            row, half = divmod(int(table[octant, entry]), 2)
            if row < 128:
                result[octant, entry, 128 * half + row] = 1
            else:
                for copy in range(4):
                    result[octant, entry, 256 + 128 * half + 32 * copy + row - 128] = 1
    return result.astype(ml_dtypes.bfloat16)


K = 136
LB = 17
MAIN = LB * 128
DEPTH = MAIN + 640
ROWS = 158
WIDE = 17 * 128
BF16 = jnp.bfloat16
F32 = jnp.float32


def translate_kernel(src_f, src_c, lists, perm, trans, out_f, out_c, idx, v, g0, g1, r):
    step = pl.program_id(0)
    cells = out_f.shape[1]
    coarse_cells = out_c.shape[1]

    @pl.when(step == 0)
    def _():
        for o in range(8):
            both = jnp.dot(lists[o], perm[o], preferred_element_type=F32)
            idx[16 * o : 16 * o + 16] = (both[:16] * 64.0 + both[16:]).astype(jnp.int32) - 1
        v[MAIN + LB * 32 :, :] = jnp.zeros((DEPTH - MAIN - LB * 32, WIDE), BF16)

    first = jnp.where(step < 8, 16 * step, MAIN + 16 * (step - 8))
    stride = jnp.where(step < 8, 128, 32)
    lane = lax.broadcasted_iota(jnp.int32, (16, 128), 1)
    live = (lax.broadcasted_iota(jnp.int32, (16, 128), 0) + 16 * step) < ROWS
    bits = [(lane // (8 << b)) % 2 == 1 for b in range(4)]

    def group(g, carry):
        base = pl.multiple_of(g * WIDE, 128)
        d = [jnp.where(live, trans[:, pl.ds(base + 128 * j, 128)], 0.0) for j in range(17)]
        for b in range(4):
            d = [jnp.where(bits[b], d[(m + (1 << b)) % 17], d[m]) for m in range(17)]
        column = pl.multiple_of(g * 128, 128)
        for lb in range(17):
            piece = d[-lb % 17]
            turn = (-8 * lb) % 128
            if turn:
                piece = pltpu.roll(piece, turn, 1)
            row = pl.multiple_of(first + lb * stride, 16)
            v[pl.ds(row, 16), pl.ds(column, 128)] = piece
        return carry

    lax.fori_loop(0, 17, group, 0)

    quarter = lax.broadcasted_iota(jnp.int32, (16, 128), 1) // 32

    def fetch_pair(src, low_row, high_row, out_row):
        places = lax.broadcasted_iota(jnp.int32, (src.shape[1], 512), 0)
        both = []
        for place in (low_row, high_row):
            hot = jnp.where(places == idx[pl.ds(place, 1), :], 1.0, 0.0).astype(BF16)
            both.append(jnp.dot(src[...], hot, preferred_element_type=F32))
        tiles = [
            jnp.concatenate([x[8 * lb : 8 * lb + 8] for x in both], axis=0) for lb in range(LB)
        ]
        rows = pl.ds(pl.multiple_of(out_row, 16), 16)
        for half, g in ((0, g0), (1, g1)):
            for lb in range(LB):
                g[rows, 128 * lb : 128 * lb + 128] = tiles[lb][:, 128 * half : 128 * half + 128].astype(BF16)
            for m in range(5):
                total = jnp.zeros((16, 128), F32)
                for j in range(4):
                    if 4 * m + j < LB:
                        part = tiles[4 * m + j][:, 256 + 128 * half : 384 + 128 * half]
                        total = jnp.where(quarter == j, part, total)
                g[rows, MAIN + 128 * m : MAIN + 128 * m + 128] = total.astype(BF16)

    @pl.when(step < cells // 8)
    def _():
        def pair(i, carry):
            fetch_pair(src_f, 32 * i + step, 32 * i + 16 + step, 64 * step + 16 * i)
            return carry

        lax.fori_loop(0, 4, pair, 0)

    @pl.when(step == 8)
    def _():
        def pair(i, carry):
            fetch_pair(src_c, 32 * i + 8, 32 * i + 24, 8 * cells + 16 * i)
            return carry

        lax.fori_loop(0, coarse_cells // 2, pair, 0)

    @pl.when(step == 9)
    def _():
        def product(g, from_column, to_column, width):
            x = jnp.dot(g[...], v[:, pl.ds(from_column, width)], preferred_element_type=F32)
            same = (
                lax.broadcasted_iota(jnp.int32, x.shape, 0) % 8
                == lax.broadcasted_iota(jnp.int32, x.shape, 1) % 8
            )
            x = jnp.where(same, x, 0.0).reshape(x.shape[0] // 8, 8, width).sum(axis=1)
            r[:, pl.ds(to_column, width)] = x

        def low(n, carry):
            product(g0, pl.multiple_of(256 * n, 128), pl.multiple_of(256 * n, 128), 256)
            return carry

        def high(n, carry):
            product(g1, pl.multiple_of(1152 + 256 * n, 128), pl.multiple_of(1280 + 256 * n, 128), 256)
            return carry

        lax.fori_loop(0, 4, low, 0)
        lax.fori_loop(0, 4, high, 0)
        product(g0, 1024, 1024, 128)
        product(g1, 1024, 1152, 128)
        column = lax.broadcasted_iota(jnp.int32, (K, 2304), 1)
        k = jnp.where(column < 1152, column // 8, (column - 128) // 8 - K)
        hit = jnp.where(k == lax.broadcasted_iota(jnp.int32, (K, 2304), 0), 1.0, 0.0)
        out = lax.dot_general(
            hit, r[...], (((1,), (1,)), ((), ())), precision=lax.Precision.HIGHEST,
            preferred_element_type=F32,
        )
        out_f[...] = out[:, :cells]
        out_c[...] = out[:, cells:]


def translate(src_f, src_c, lists, perm, translators, cells, coarse_cells):
    total = cells + coarse_cells

    def whole(x):
        return pl.BlockSpec(x.shape, lambda s: (0,) * x.ndim)

    return pl.pallas_call(
        translate_kernel,
        grid=(10,),
        in_specs=[
            whole(src_f), whole(src_c), whole(lists), whole(perm),
            pl.BlockSpec((16, translators.shape[1]), lambda s: (s, 0)),
        ],
        out_specs=[
            pl.BlockSpec((K, cells), lambda s: (0, 0)),
            pl.BlockSpec((K, coarse_cells), lambda s: (0, 0)),
        ],
        out_shape=[
            jax.ShapeDtypeStruct((K, cells), F32),
            jax.ShapeDtypeStruct((K, coarse_cells), F32),
        ],
        scratch_shapes=[
            pltpu.VMEM((128, 512), jnp.int32),
            pltpu.VMEM((DEPTH, WIDE), BF16),
            pltpu.VMEM((8 * total, DEPTH), BF16),
            pltpu.VMEM((8 * total, DEPTH), BF16),
            pltpu.VMEM((total, 2304), F32),
        ],
        compiler_params=pltpu.CompilerParams(vmem_limit_bytes=56 * 2**20),
    )(src_f, src_c, lists, perm, translators)


def list_rows(fine_lists, fine_flags, coarse_lists, coarse_flags):
    fine = jnp.where(fine_flags == 1, fine_lists + 1, 0).reshape(189, 8, 8)
    coarse = jnp.where(coarse_flags == 1, coarse_lists + 1, 0).reshape(189, 1, 8)
    both = jnp.concatenate([fine, coarse, jnp.zeros((189, 7, 8), jnp.int32)], axis=1)
    both = jnp.transpose(both, (2, 1, 0))
    return jnp.concatenate([both // 64, both % 64], axis=1).astype(BF16)


def fetch(levels):
    upward = jnp.concatenate(
        [jnp.take(level[0], level[2][0, 0], axis=1) for level in levels], axis=1
    )
    downward = jnp.concatenate(
        [jnp.take(level[0], level[2][0, 1], axis=1) for level in levels], axis=1
    )
    below = passed_along(upward, "gx", 1)
    above = passed_along(downward, "gx", -1)
    row_parts = jnp.concatenate(
        [jnp.take(level[0], level[1][0], axis=1) for level in levels], axis=2
    )
    received = lax.all_to_all(row_parts, "gy", split_axis=1, concat_axis=1, tiled=True)
    buffers = []
    side_start = 0
    row_start = 0
    for level in levels:
        cap = level[1].shape[2]
        side = level[2].shape[2]
        row = received[:, :, row_start : row_start + cap].reshape(level[0].shape[0], -1)
        row_start += cap
        sides = slice(side_start, side_start + side)
        side_start += side
        buffers.append(jnp.concatenate([level[0], row, below[:, sides], above[:, sides]], axis=1))
    return buffers


def shards(
    multipoles,
    parent_ops,
    translators,
    fine_exports,
    fine_sides,
    fine_lists,
    fine_flags,
    coarse_exports,
    coarse_sides,
    coarse_lists,
    coarse_flags,
):
    coeffs = multipoles.shape[0]
    octant_ops = parent_ops.reshape(8, coeffs, coeffs)
    children = multipoles.reshape(coeffs, -1, 8)
    coarse = jnp.einsum(
        "okl,lqo->kq", octant_ops, children, preferred_element_type=jnp.float32
    ).astype(jnp.bfloat16)
    fine_buffer, coarse_buffer = fetch(
        [(multipoles, fine_exports, fine_sides), (coarse, coarse_exports, coarse_sides)]
    )
    lists = list_rows(fine_lists, fine_flags, coarse_lists, coarse_flags)
    perm = jnp.asarray(entry_to_lane())
    return tuple(
        translate(
            fine_buffer, coarse_buffer, lists, perm, translators,
            fine_lists.shape[1], coarse_lists.shape[1],
        )
    )


def solution(mesh):
    return jax.shard_map(
        shards,
        mesh=mesh,
        in_specs=(
            P(None, ("gx", "gy")),
            P(),
            P(),
            P(("gx", "gy"), None, None),
            P(("gx", "gy"), None, None),
            P(None, ("gx", "gy")),
            P(None, ("gx", "gy")),
            P(("gx", "gy"), None, None),
            P(("gx", "gy"), None, None),
            P(None, ("gx", "gy")),
            P(None, ("gx", "gy")),
        ),
        out_specs=(P(None, ("gx", "gy")), P(None, ("gx", "gy"))),
        check_vma=False,
    )
```

```python
import functools

import jax
import jax.numpy as jnp
import ml_dtypes
import numpy as np
from jax import lax
from jax.experimental import pallas as pl
from jax.experimental.pallas import tpu as pltpu
from jax.sharding import PartitionSpec as P


def direction_table():
    far_offsets = {}
    for shift_x in range(-3, 4):
        for shift_y in range(-3, 4):
            for shift_z in range(-3, 4):
                if max(abs(shift_x), abs(shift_y), abs(shift_z)) > 1:
                    far_offsets[shift_x, shift_y, shift_z] = len(far_offsets)
    result = np.zeros((8, 189), np.int32)
    for octant in range(8):
        own_x, own_y, own_z = (octant % 2, octant // 2 % 2, octant // 4)
        column = 0
        for parent_x in (-1, 0, 1):
            for parent_y in (-1, 0, 1):
                for parent_z in (-1, 0, 1):
                    for child in range(8):
                        step_x = 2 * parent_x + child % 2 - own_x
                        step_y = 2 * parent_y + child // 2 % 2 - own_y
                        step_z = 2 * parent_z + child // 4 - own_z
                        if max(abs(step_x), abs(step_y), abs(step_z)) > 1:
                            result[octant, column] = far_offsets[step_x, step_y, step_z]
                            column = column + 1
    return result


def entry_to_lane():
    table = direction_table()
    result = np.zeros((8, 189, 512), np.float32)
    for octant in range(8):
        for entry in range(189):
            row, half = divmod(int(table[octant, entry]), 2)
            if row < 128:
                result[octant, entry, 128 * half + row] = 1
            else:
                for copy in range(4):
                    result[octant, entry, 256 + 128 * half + 32 * copy + row - 128] = 1
    return result.astype(ml_dtypes.bfloat16)


K = 136
LB = 17
MAIN = LB * 128
DEPTH = MAIN + 640
ROWS = 158
WIDE = 17 * 128
BF16 = jnp.bfloat16
F32 = jnp.float32


def translate_kernel(src_f, src_c, lists, perm, trans, out_f, out_c, idx, v, g0, g1, r):
    step = pl.program_id(0)
    cells = out_f.shape[1]
    coarse_cells = out_c.shape[1]

    @pl.when(step == 0)
    def _():
        for o in range(8):
            both = jnp.dot(lists[o], perm[o], preferred_element_type=F32)
            idx[16 * o : 16 * o + 16] = (both[:16] * 64.0 + both[16:]).astype(jnp.int32) - 1
        v[MAIN + LB * 32 :, :] = jnp.zeros((DEPTH - MAIN - LB * 32, WIDE), BF16)

    first = jnp.where(step < 8, 16 * step, MAIN + 16 * (step - 8))
    stride = jnp.where(step < 8, 128, 32)
    lane = lax.broadcasted_iota(jnp.int32, (16, 128), 1)
    live = (lax.broadcasted_iota(jnp.int32, (16, 128), 0) + 16 * step) < ROWS
    bits = [(lane // (8 << b)) % 2 == 1 for b in range(4)]

    def group(g, carry):
        base = pl.multiple_of(g * WIDE, 128)
        d = [jnp.where(live, trans[:, pl.ds(base + 128 * j, 128)], 0.0) for j in range(17)]
        for b in range(4):
            d = [jnp.where(bits[b], d[(m + (1 << b)) % 17], d[m]) for m in range(17)]
        column = pl.multiple_of(g * 128, 128)
        for lb in range(17):
            piece = d[-lb % 17]
            turn = (-8 * lb) % 128
            if turn:
                piece = pltpu.roll(piece, turn, 1)
            row = pl.multiple_of(first + lb * stride, 16)
            v[pl.ds(row, 16), pl.ds(column, 128)] = piece
        return carry

    lax.fori_loop(0, 17, group, 0)

    quarter = lax.broadcasted_iota(jnp.int32, (16, 128), 1) // 32

    def fetch_pair(src, low_row, high_row, out_row):
        places = lax.broadcasted_iota(jnp.int32, (src.shape[1], 512), 0)
        both = []
        for place in (low_row, high_row):
            hot = jnp.where(places == idx[pl.ds(place, 1), :], 1.0, 0.0).astype(BF16)
            both.append(jnp.dot(src[...], hot, preferred_element_type=F32))
        tiles = [
            jnp.concatenate([x[8 * lb : 8 * lb + 8] for x in both], axis=0) for lb in range(LB)
        ]
        rows = pl.ds(pl.multiple_of(out_row, 16), 16)
        for half, g in ((0, g0), (1, g1)):
            for lb in range(LB):
                g[rows, 128 * lb : 128 * lb + 128] = tiles[lb][:, 128 * half : 128 * half + 128].astype(BF16)
            for m in range(5):
                total = jnp.zeros((16, 128), F32)
                for j in range(4):
                    if 4 * m + j < LB:
                        part = tiles[4 * m + j][:, 256 + 128 * half : 384 + 128 * half]
                        total = jnp.where(quarter == j, part, total)
                g[rows, MAIN + 128 * m : MAIN + 128 * m + 128] = total.astype(BF16)

    @pl.when(step < cells // 8)
    def _():
        def pair(i, carry):
            fetch_pair(src_f, 32 * i + step, 32 * i + 16 + step, 64 * step + 16 * i)
            return carry

        lax.fori_loop(0, 4, pair, 0)

    @pl.when(step == 8)
    def _():
        def pair(i, carry):
            fetch_pair(src_c, 32 * i + 8, 32 * i + 24, 8 * cells + 16 * i)
            return carry

        lax.fori_loop(0, coarse_cells // 2, pair, 0)

    @pl.when(step == 9)
    def _():
        def product(g, from_column, to_column, width):
            x = jnp.dot(g[...], v[:, pl.ds(from_column, width)], preferred_element_type=F32)
            same = (
                lax.broadcasted_iota(jnp.int32, x.shape, 0) % 8
                == lax.broadcasted_iota(jnp.int32, x.shape, 1) % 8
            )
            x = jnp.where(same, x, 0.0).reshape(x.shape[0] // 8, 8, width).sum(axis=1)
            r[:, pl.ds(to_column, width)] = x

        def low(n, carry):
            product(g0, pl.multiple_of(256 * n, 128), pl.multiple_of(256 * n, 128), 256)
            return carry

        def high(n, carry):
            product(g1, pl.multiple_of(1152 + 256 * n, 128), pl.multiple_of(1280 + 256 * n, 128), 256)
            return carry

        lax.fori_loop(0, 4, low, 0)
        lax.fori_loop(0, 4, high, 0)
        product(g0, 1024, 1024, 128)
        product(g1, 1024, 1152, 128)
        column = lax.broadcasted_iota(jnp.int32, (K, 2304), 1)
        k = jnp.where(column < 1152, column // 8, (column - 128) // 8 - K)
        hit = jnp.where(k == lax.broadcasted_iota(jnp.int32, (K, 2304), 0), 1.0, 0.0)
        out = lax.dot_general(
            hit, r[...], (((1,), (1,)), ((), ())), precision=lax.Precision.HIGHEST,
            preferred_element_type=F32,
        )
        out_f[...] = out[:, :cells]
        out_c[...] = out[:, cells:]


def translate(src_f, src_c, lists, perm, translators, cells, coarse_cells):
    total = cells + coarse_cells

    def whole(x):
        return pl.BlockSpec(x.shape, lambda s: (0,) * x.ndim)

    return pl.pallas_call(
        translate_kernel,
        grid=(10,),
        in_specs=[
            whole(src_f), whole(src_c), whole(lists), whole(perm),
            pl.BlockSpec((16, translators.shape[1]), lambda s: (s, 0)),
        ],
        out_specs=[
            pl.BlockSpec((K, cells), lambda s: (0, 0)),
            pl.BlockSpec((K, coarse_cells), lambda s: (0, 0)),
        ],
        out_shape=[
            jax.ShapeDtypeStruct((K, cells), F32),
            jax.ShapeDtypeStruct((K, coarse_cells), F32),
        ],
        scratch_shapes=[
            pltpu.VMEM((128, 512), jnp.int32),
            pltpu.VMEM((DEPTH, WIDE), BF16),
            pltpu.VMEM((8 * total, DEPTH), BF16),
            pltpu.VMEM((8 * total, DEPTH), BF16),
            pltpu.VMEM((total, 2304), F32),
        ],
        compiler_params=pltpu.CompilerParams(vmem_limit_bytes=56 * 2**20),
    )(src_f, src_c, lists, perm, translators)


def round_up(count):
    return -(-count // 16) * 16


def list_rows(fine_lists, fine_flags, coarse_lists, coarse_flags, own, cap, peers, side):
    row = coarse_lists - own
    sides = row - cap * peers
    slot = round_up(own)
    row_slot = slot + round_up(cap) * (row // cap) + row % cap
    side_slot = slot + round_up(cap) * peers + round_up(side) * (sides // side) + sides % side
    coarse_places = jnp.where(row < 0, coarse_lists, jnp.where(sides < 0, row_slot, side_slot))
    fine = jnp.where(fine_flags == 1, fine_lists + 1, 0).reshape(189, 8, 8)
    coarse = jnp.where(coarse_flags == 1, coarse_places + 1, 0).reshape(189, 1, 8)
    both = jnp.concatenate([fine, coarse, jnp.zeros((189, 7, 8), jnp.int32)], axis=1)
    both = jnp.transpose(both, (2, 1, 0))
    return jnp.concatenate([both // 64, both % 64], axis=1).astype(BF16)


def exchange_kernel(
    n_gx, n_gy, plan, sel, mult, out_f, out_c, picked, buf_f, buf_c, send_sems, recv_sems
):
    i = lax.axis_index("gx")
    j = lax.axis_index("gy")
    mesh_ids = pl.DeviceIdType.MESH
    barrier = pltpu.get_barrier_semaphore()
    for d in range(1, n_gy):
        peer = lax.rem(j + d, n_gy)
        pl.semaphore_signal(barrier, inc=1, device_id=(i, peer), device_id_type=mesh_ids)

    @pl.when(i > 0)
    def _():
        pl.semaphore_signal(barrier, inc=1, device_id=(i - 1, j), device_id_type=mesh_ids)

    @pl.when(i < n_gx - 1)
    def _():
        pl.semaphore_signal(barrier, inc=1, device_id=(i + 1, j), device_id_type=mesh_ids)

    hot = jnp.where(
        sel[...] == lax.broadcasted_iota(jnp.int32, (sel.shape[0], mult.shape[1]), 1), 1.0, 0.0
    ).astype(BF16)
    values = lax.dot_general(
        hot, mult[...], (((1,), (1,)), ((), ())), preferred_element_type=F32
    ).astype(BF16)
    picked[...] = values
    pl.semaphore_wait(barrier, n_gy - 1 + jnp.where(i > 0, 1, 0) + jnp.where(i < n_gx - 1, 1, 0))

    def row(start):
        return pl.multiple_of(start, 16)

    copies = []
    for level, (buf, own, cap, side, base) in enumerate(zip((buf_f, buf_c), *plan)):
        for d in range(1, n_gy):
            peer = lax.rem(j + d, n_gy)
            copy = pltpu.make_async_remote_copy(
                src_ref=picked.at[pl.ds(row(base + own + cap * peer), cap)],
                dst_ref=buf.at[pl.ds(row(own + cap * j), cap)],
                send_sem=send_sems.at[level, d],
                recv_sem=recv_sems.at[level, d],
                device_id=(i, peer),
                device_id_type=mesh_ids,
            )
            copy.start()
            copies.append(copy)
    neighbours = []
    for level, (buf, own, cap, side, base) in enumerate(zip((buf_f, buf_c), *plan)):
        first = own + cap * n_gy
        for turn, there in ((0, i + 1), (1, i - 1)):
            copy = pltpu.make_async_remote_copy(
                src_ref=picked.at[pl.ds(base + first + side * turn, side)],
                dst_ref=buf.at[pl.ds(first + side * turn, side)],
                send_sem=send_sems.at[level, n_gy + turn],
                recv_sem=recv_sems.at[level, n_gy + turn],
                device_id=(there, j),
                device_id_type=mesh_ids,
            )
            sends = (i < n_gx - 1) if turn == 0 else (i > 0)
            receives = (i > 0) if turn == 0 else (i < n_gx - 1)
            neighbours.append((copy, sends, receives))
            pl.when(sends)(copy.start)

            @pl.when(jnp.logical_not(receives))
            def _(buf=buf, start=first + side * turn, side=side):
                buf[pl.ds(start, side), :] = jnp.zeros((side, K), BF16)

        buf[:own, :] = picked[base : base + own, :]
        buf[pl.ds(row(own + cap * j), cap), :] = picked[pl.ds(row(base + own + cap * j), cap), :]
    for copy in copies:
        copy.wait_send()
        copy.wait_recv()
    for copy, sends, receives in neighbours:
        pl.when(sends)(copy.wait_send)
        pl.when(receives)(copy.wait_recv)
    out_f[...] = buf_f[...].T
    out_c[...] = buf_c[...].T


def exchange(mult, coarse, fine_exports, fine_sides, coarse_exports, coarse_sides):
    n_gx, n_gy = lax.axis_size("gx"), lax.axis_size("gy")
    own_f, own_c = mult.shape[1], coarse.shape[1]

    def rows(own, exports, sides, offset):
        parts = [jnp.arange(own, dtype=jnp.int32)[None], exports[0], sides[0]]
        padded = [
            jnp.pad(p + offset, ((0, 0), (0, round_up(p.shape[1]) - p.shape[1])), constant_values=-1)
            for p in parts
        ]
        return jnp.concatenate([p.reshape(-1) for p in padded])

    sel_f = rows(own_f, fine_exports, fine_sides, 0)
    sel_c = rows(own_c, coarse_exports, coarse_sides, own_f)
    sel = jnp.concatenate([sel_f, sel_c])[:, None]
    both = jnp.concatenate([mult, coarse], axis=1)
    plan = (
        (round_up(own_f), round_up(own_c)),
        (round_up(fine_exports.shape[2]), round_up(coarse_exports.shape[2])),
        (round_up(fine_sides.shape[2]), round_up(coarse_sides.shape[2])),
        (0, sel_f.shape[0]),
    )
    vmem = pl.BlockSpec(memory_space=pltpu.VMEM)
    return pl.pallas_call(
        functools.partial(exchange_kernel, n_gx, n_gy, plan),
        in_specs=[vmem, vmem],
        out_specs=[vmem, vmem],
        out_shape=[
            jax.ShapeDtypeStruct((K, sel_f.shape[0]), BF16),
            jax.ShapeDtypeStruct((K, sel_c.shape[0]), BF16),
        ],
        scratch_shapes=[
            pltpu.VMEM((sel.shape[0], K), BF16),
            pltpu.VMEM((sel_f.shape[0], K), BF16),
            pltpu.VMEM((sel_c.shape[0], K), BF16),
            pltpu.SemaphoreType.DMA((2, n_gy + 2)),
            pltpu.SemaphoreType.DMA((2, n_gy + 2)),
        ],
        compiler_params=pltpu.CompilerParams(
            collective_id=0, has_side_effects=True, vmem_limit_bytes=32 * 2**20
        ),
    )(sel, both)


def shards(
    multipoles,
    parent_ops,
    translators,
    fine_exports,
    fine_sides,
    fine_lists,
    fine_flags,
    coarse_exports,
    coarse_sides,
    coarse_lists,
    coarse_flags,
):
    coeffs = multipoles.shape[0]
    octant_ops = parent_ops.reshape(8, coeffs, coeffs)
    children = multipoles.reshape(coeffs, -1, 8)
    coarse = jnp.einsum(
        "okl,lqo->kq", octant_ops, children, preferred_element_type=jnp.float32
    ).astype(jnp.bfloat16)
    fine_buffer, coarse_buffer = exchange(
        multipoles, coarse, fine_exports, fine_sides, coarse_exports, coarse_sides
    )
    lists = list_rows(
        fine_lists, fine_flags, coarse_lists, coarse_flags,
        coarse.shape[1], coarse_exports.shape[2], coarse_exports.shape[1], coarse_sides.shape[2],
    )
    perm = jnp.asarray(entry_to_lane())
    return tuple(
        translate(
            fine_buffer, coarse_buffer, lists, perm, translators,
            fine_lists.shape[1], coarse_lists.shape[1],
        )
    )


def solution(mesh):
    return jax.shard_map(
        shards,
        mesh=mesh,
        in_specs=(
            P(None, ("gx", "gy")),
            P(),
            P(),
            P(("gx", "gy"), None, None),
            P(("gx", "gy"), None, None),
            P(None, ("gx", "gy")),
            P(None, ("gx", "gy")),
            P(("gx", "gy"), None, None),
            P(("gx", "gy"), None, None),
            P(None, ("gx", "gy")),
            P(None, ("gx", "gy")),
        ),
        out_specs=(P(None, ("gx", "gy")), P(None, ("gx", "gy"))),
        check_vma=False,
    )
```

```python
import functools

import jax
import jax.numpy as jnp
import ml_dtypes
import numpy as np
from jax import lax
from jax.experimental import pallas as pl
from jax.experimental.pallas import tpu as pltpu
from jax.sharding import PartitionSpec as P


def direction_table():
    far_offsets = {}
    for shift_x in range(-3, 4):
        for shift_y in range(-3, 4):
            for shift_z in range(-3, 4):
                if max(abs(shift_x), abs(shift_y), abs(shift_z)) > 1:
                    far_offsets[shift_x, shift_y, shift_z] = len(far_offsets)
    result = np.zeros((8, 189), np.int32)
    for octant in range(8):
        own_x, own_y, own_z = (octant % 2, octant // 2 % 2, octant // 4)
        column = 0
        for parent_x in (-1, 0, 1):
            for parent_y in (-1, 0, 1):
                for parent_z in (-1, 0, 1):
                    for child in range(8):
                        step_x = 2 * parent_x + child % 2 - own_x
                        step_y = 2 * parent_y + child // 2 % 2 - own_y
                        step_z = 2 * parent_z + child // 4 - own_z
                        if max(abs(step_x), abs(step_y), abs(step_z)) > 1:
                            result[octant, column] = far_offsets[step_x, step_y, step_z]
                            column = column + 1
    return result


def entry_to_lane():
    table = direction_table()
    result = np.zeros((8, 189, 512), np.float32)
    for octant in range(8):
        for entry in range(189):
            row, half = divmod(int(table[octant, entry]), 2)
            if row < 128:
                result[octant, entry, 128 * half + row] = 1
            else:
                for copy in range(4):
                    result[octant, entry, 256 + 128 * half + 32 * copy + row - 128] = 1
    return result.astype(ml_dtypes.bfloat16)


K = 136
LB = 17
MAIN = LB * 128
DEPTH = MAIN + 640
ROWS = 158
WIDE = 17 * 128
BF16 = jnp.bfloat16
F32 = jnp.float32


def translate_kernel(
    jumps, src_f, src_c, fine_lists, fine_flags, coarse_lists, coarse_flags, perm, trans,
    out_f, out_c, idx, v, g0, g1, r,
):
    step = pl.program_id(0)
    cells = out_f.shape[0]
    coarse_cells = out_c.shape[0]

    @pl.when(step == 0)
    def _():
        places = coarse_lists[...]
        moved = places
        for start, gap in jumps:
            moved = moved + jnp.where(places >= start, gap, 0)
        fine = jnp.where(fine_flags[...] == 1, fine_lists[...] + 1, 0)
        coarse = jnp.where(coarse_flags[...] == 1, moved + 1, 0)
        total = cells + coarse_cells
        both = jnp.concatenate([fine, coarse], axis=0)
        digits = jnp.concatenate([both >> 6, both & 63], axis=0).astype(F32).astype(BF16)
        octant = lax.broadcasted_iota(jnp.int32, (total, 512), 0) % 8
        found = jnp.zeros((total, 512), F32)
        for o in range(8):
            x = jnp.dot(digits, perm[o], preferred_element_type=F32)
            found = jnp.where(octant == o, x[:total] * 64.0 + x[total:], found)
        idx[...] = found.astype(jnp.int32) - 1
        v[MAIN + LB * 32 :, :] = jnp.zeros((DEPTH - MAIN - LB * 32, WIDE), BF16)

    first = jnp.where(step < 8, 16 * step, MAIN + 16 * (step - 8))
    stride = jnp.where(step < 8, 128, 32)
    lane = lax.broadcasted_iota(jnp.int32, (16, 128), 1)
    live = (lax.broadcasted_iota(jnp.int32, (16, 128), 0) + 16 * step) < ROWS
    bits = [(lane // (8 << b)) % 2 == 1 for b in range(4)]

    def group(g):
        base = g * WIDE
        d = [jnp.where(live, trans[:, base + 128 * j : base + 128 * j + 128], 0.0) for j in range(17)]
        for b in range(4):
            d = [jnp.where(bits[b], d[(m + (1 << b)) % 17], d[m]) for m in range(17)]
        for lb in range(17):
            piece = d[-lb % 17]
            turn = (-8 * lb) % 128
            if turn:
                piece = pltpu.roll(piece, turn, 1)
            row = pl.multiple_of(first + lb * stride, 16)
            v[pl.ds(row, 16), 128 * g : 128 * g + 128] = piece


    quarter = lax.broadcasted_iota(jnp.int32, (16, 128), 1) // 32

    def fetch_pair(src, low_row, high_row, out_row):
        places = lax.broadcasted_iota(jnp.int32, (src.shape[1], 512), 0).astype(jnp.int16)
        both = []
        for place in (low_row, high_row):
            wanted = jnp.broadcast_to(idx[pl.ds(place, 1), :], (16, 512)).astype(jnp.int16)
            wanted = jnp.broadcast_to(wanted[None], (src.shape[1] // 16, 16, 512))
            hot = jnp.where(
                places == wanted.reshape(src.shape[1], 512), jnp.ones((), BF16), jnp.zeros((), BF16)
            )
            both.append(jnp.dot(src[...], hot, preferred_element_type=F32))
        tiles = [
            jnp.concatenate([x[8 * lb : 8 * lb + 8] for x in both], axis=0) for lb in range(LB)
        ]
        rows = pl.ds(pl.multiple_of(out_row, 16), 16)
        for half, g in ((0, g0), (1, g1)):
            for lb in range(LB):
                g[rows, 128 * lb : 128 * lb + 128] = tiles[lb][:, 128 * half : 128 * half + 128].astype(BF16)
            for m in range(5):
                total = jnp.zeros((16, 128), F32)
                for j in range(4):
                    if 4 * m + j < LB:
                        part = tiles[4 * m + j][:, 256 + 128 * half : 384 + 128 * half]
                        total = jnp.where(quarter == j, part, total)
                g[rows, MAIN + 128 * m : MAIN + 128 * m + 128] = total.astype(BF16)

    @pl.when(step >= 8)
    def _():
        for g in range(17):
            group(g)

    @pl.when(step < 8)
    def _():
        for g in range(17):
            group(g)
        for i in range(4):
            fetch_pair(src_f, 8 * step + 2 * i, 8 * step + 2 * i + 1, 64 * step + 16 * i)

    @pl.when(step == 8)
    def _():
        for i in range(coarse_cells // 2):
            fetch_pair(src_c, cells + 2 * i, cells + 2 * i + 1, 8 * cells + 16 * i)

    @pl.when(step == 9)
    def _():
        def product(g, from_column, to_column, width):
            x = jnp.dot(g[...], v[:, pl.ds(from_column, width)], preferred_element_type=F32)
            same = (
                lax.broadcasted_iota(jnp.int32, x.shape, 0) % 8
                == lax.broadcasted_iota(jnp.int32, x.shape, 1) % 8
            )
            x = jnp.where(same, x, 0.0).reshape(x.shape[0] // 8, 8, width).sum(axis=1)
            r[:, pl.ds(to_column, width)] = x

        def low(n, carry):
            product(g0, pl.multiple_of(256 * n, 128), pl.multiple_of(256 * n, 128), 256)
            return carry

        def high(n, carry):
            product(g1, pl.multiple_of(1152 + 256 * n, 128), pl.multiple_of(1280 + 256 * n, 128), 256)
            return carry

        lax.fori_loop(0, 4, low, 0)
        lax.fori_loop(0, 4, high, 0)
        product(g0, 1024, 1024, 128)
        product(g1, 1024, 1152, 128)
        column = lax.broadcasted_iota(jnp.int32, (K, 2304), 1)
        k = jnp.where(column < 1152, column // 8, (column - 128) // 8 - K)
        hit = jnp.where(k == lax.broadcasted_iota(jnp.int32, (K, 2304), 0), 1.0, 0.0).astype(BF16)
        out = jnp.zeros((cells + coarse_cells, K), F32)
        rest = r[...]
        for _ in range(3):
            piece = rest.astype(BF16)
            rest = rest - piece.astype(F32)
            out = out + lax.dot_general(
                piece, hit, (((1,), (1,)), ((), ())), preferred_element_type=F32
            )
        out_f[...] = out[:cells]
        out_c[...] = out[cells:]


def translate(jumps, src_f, src_c, lists, perm, translators):
    cells, coarse_cells = lists[0].shape[0], lists[2].shape[0]
    total = cells + coarse_cells

    def whole(x):
        return pl.BlockSpec(x.shape, lambda s: (0,) * x.ndim)

    return pl.pallas_call(
        functools.partial(translate_kernel, jumps),
        grid=(10,),
        in_specs=[
            whole(src_f), whole(src_c), *[whole(x) for x in lists], whole(perm),
            pl.BlockSpec((16, translators.shape[1]), lambda s: (s, 0)),
        ],
        out_specs=[
            pl.BlockSpec((cells, K), lambda s: (0, 0)),
            pl.BlockSpec((coarse_cells, K), lambda s: (0, 0)),
        ],
        out_shape=[
            jax.ShapeDtypeStruct((cells, K), F32),
            jax.ShapeDtypeStruct((coarse_cells, K), F32),
        ],
        scratch_shapes=[
            pltpu.VMEM((total, 512), jnp.int32),
            pltpu.VMEM((DEPTH, WIDE), BF16),
            pltpu.VMEM((8 * total, DEPTH), BF16),
            pltpu.VMEM((8 * total, DEPTH), BF16),
            pltpu.VMEM((total, 2304), F32),
        ],
        compiler_params=pltpu.CompilerParams(vmem_limit_bytes=56 * 2**20),
    )(src_f, src_c, *lists, perm, translators)


def round_up(count):
    return -(-count // 16) * 16


def exchange_kernel(
    n_gx, n_gy, plan, sel, mult, out_f, out_c, picked, buf_f, buf_c, send_sems, recv_sems
):
    i = lax.axis_index("gx")
    j = lax.axis_index("gy")
    mesh_ids = pl.DeviceIdType.MESH
    barrier = pltpu.get_barrier_semaphore()
    for d in range(1, n_gy):
        peer = lax.rem(j + d, n_gy)
        pl.semaphore_signal(barrier, inc=1, device_id=(i, peer), device_id_type=mesh_ids)

    @pl.when(i > 0)
    def _():
        pl.semaphore_signal(barrier, inc=1, device_id=(i - 1, j), device_id_type=mesh_ids)

    @pl.when(i < n_gx - 1)
    def _():
        pl.semaphore_signal(barrier, inc=1, device_id=(i + 1, j), device_id_type=mesh_ids)

    hot = jnp.where(
        sel[...] == lax.broadcasted_iota(jnp.int32, (sel.shape[0], mult.shape[0]), 1), 1.0, 0.0
    ).astype(BF16)
    picked[...] = jnp.dot(hot, mult[...], preferred_element_type=F32).astype(BF16)
    pl.semaphore_wait(barrier, n_gy - 1 + jnp.where(i > 0, 1, 0) + jnp.where(i < n_gx - 1, 1, 0))

    def row(start):
        return pl.multiple_of(start, 16)

    copies = []
    for level, (buf, own, cap, side, base) in enumerate(zip((buf_f, buf_c), *plan)):
        for d in range(1, n_gy):
            peer = lax.rem(j + d, n_gy)
            copy = pltpu.make_async_remote_copy(
                src_ref=picked.at[pl.ds(row(base + own + cap * peer), cap)],
                dst_ref=buf.at[pl.ds(row(own + cap * j), cap)],
                send_sem=send_sems.at[level, d],
                recv_sem=recv_sems.at[level, d],
                device_id=(i, peer),
                device_id_type=mesh_ids,
            )
            copy.start()
            copies.append(copy)
    neighbours = []
    for level, (buf, own, cap, side, base) in enumerate(zip((buf_f, buf_c), *plan)):
        first = own + cap * n_gy
        for turn, there in ((0, i + 1), (1, i - 1)):
            copy = pltpu.make_async_remote_copy(
                src_ref=picked.at[pl.ds(base + first + side * turn, side)],
                dst_ref=buf.at[pl.ds(first + side * turn, side)],
                send_sem=send_sems.at[level, n_gy + turn],
                recv_sem=recv_sems.at[level, n_gy + turn],
                device_id=(there, j),
                device_id_type=mesh_ids,
            )
            sends = (i < n_gx - 1) if turn == 0 else (i > 0)
            receives = (i > 0) if turn == 0 else (i < n_gx - 1)
            neighbours.append((copy, sends, receives))
            pl.when(sends)(copy.start)

            @pl.when(jnp.logical_not(receives))
            def _(buf=buf, start=first + side * turn, side=side):
                buf[pl.ds(start, side), :] = jnp.zeros((side, K), BF16)

        buf[:own, :] = picked[base : base + own, :]
        buf[pl.ds(row(own + cap * j), cap), :] = picked[pl.ds(row(base + own + cap * j), cap), :]
    for copy in copies:
        copy.wait_send()
        copy.wait_recv()
    for copy, sends, receives in neighbours:
        pl.when(sends)(copy.wait_send)
        pl.when(receives)(copy.wait_recv)
    out_f[...] = buf_f[...].T
    out_c[...] = buf_c[...].T


def exchange(mult, coarse, fine_exports, fine_sides, coarse_exports, coarse_sides):
    n_gx, n_gy = lax.axis_size("gx"), lax.axis_size("gy")
    own_f, own_c = mult.shape[0], coarse.shape[0]

    def rows(own, exports, sides, offset):
        parts = [jnp.arange(own, dtype=jnp.int32)[None], exports[0], sides[0]]
        padded = [
            jnp.pad(p + offset, ((0, 0), (0, round_up(p.shape[1]) - p.shape[1])), constant_values=-1)
            for p in parts
        ]
        return jnp.concatenate([p.reshape(-1) for p in padded])

    sel_f = rows(own_f, fine_exports, fine_sides, 0)
    sel_c = rows(own_c, coarse_exports, coarse_sides, own_f)
    sel = jnp.concatenate([sel_f, sel_c])[:, None]
    both = jnp.concatenate([mult, coarse], axis=0)
    plan = (
        (round_up(own_f), round_up(own_c)),
        (round_up(fine_exports.shape[2]), round_up(coarse_exports.shape[2])),
        (round_up(fine_sides.shape[2]), round_up(coarse_sides.shape[2])),
        (0, sel_f.shape[0]),
    )
    vmem = pl.BlockSpec(memory_space=pltpu.VMEM)
    return pl.pallas_call(
        functools.partial(exchange_kernel, n_gx, n_gy, plan),
        in_specs=[vmem, vmem],
        out_specs=[vmem, vmem],
        out_shape=[
            jax.ShapeDtypeStruct((K, sel_f.shape[0]), BF16),
            jax.ShapeDtypeStruct((K, sel_c.shape[0]), BF16),
        ],
        scratch_shapes=[
            pltpu.VMEM((sel.shape[0], K), BF16),
            pltpu.VMEM((sel_f.shape[0], K), BF16),
            pltpu.VMEM((sel_c.shape[0], K), BF16),
            pltpu.SemaphoreType.DMA((2, n_gy + 2)),
            pltpu.SemaphoreType.DMA((2, n_gy + 2)),
        ],
        compiler_params=pltpu.CompilerParams(
            collective_id=0, has_side_effects=True, vmem_limit_bytes=32 * 2**20
        ),
    )(sel, both)


def shards(
    multipoles,
    parent_ops,
    translators,
    fine_exports,
    fine_sides,
    fine_lists,
    fine_flags,
    coarse_exports,
    coarse_sides,
    coarse_lists,
    coarse_flags,
):
    coeffs = multipoles.shape[0]
    octant_ops = parent_ops.reshape(8, coeffs, coeffs)
    children = multipoles.T.reshape(-1, 8, coeffs)
    coarse = jnp.einsum(
        "okl,qol->qk", octant_ops, children, preferred_element_type=jnp.float32
    ).astype(jnp.bfloat16)
    fine_buffer, coarse_buffer = exchange(
        multipoles.T, coarse, fine_exports, fine_sides, coarse_exports, coarse_sides
    )
    own = coarse.shape[0]
    peers, cap = coarse_exports.shape[1:]
    side = coarse_sides.shape[2]
    jumps = [(own, round_up(own) - own)]
    jumps += [(own + cap * p, round_up(cap) - cap) for p in range(1, peers + 1)]
    jumps += [(own + cap * peers + side, round_up(side) - side)]
    lists = [x.T for x in (fine_lists, fine_flags, coarse_lists, coarse_flags)]
    perm = jnp.asarray(entry_to_lane())
    fine, coarse = translate(jumps, fine_buffer, coarse_buffer, lists, perm, translators)
    return fine.T, coarse.T


def solution(mesh):
    return jax.shard_map(
        shards,
        mesh=mesh,
        in_specs=(
            P(None, ("gx", "gy")),
            P(),
            P(),
            P(("gx", "gy"), None, None),
            P(("gx", "gy"), None, None),
            P(None, ("gx", "gy")),
            P(None, ("gx", "gy")),
            P(("gx", "gy"), None, None),
            P(("gx", "gy"), None, None),
            P(None, ("gx", "gy")),
            P(None, ("gx", "gy")),
        ),
        out_specs=(P(None, ("gx", "gy")), P(None, ("gx", "gy"))),
        check_vma=False,
    )
```

```python
import functools

import jax
import jax.numpy as jnp
import ml_dtypes
import numpy as np
from jax import lax
from jax.experimental import pallas as pl
from jax.experimental.pallas import tpu as pltpu
from jax.sharding import PartitionSpec as P


def direction_table():
    far_offsets = {}
    for shift_x in range(-3, 4):
        for shift_y in range(-3, 4):
            for shift_z in range(-3, 4):
                if max(abs(shift_x), abs(shift_y), abs(shift_z)) > 1:
                    far_offsets[shift_x, shift_y, shift_z] = len(far_offsets)
    result = np.zeros((8, 189), np.int32)
    for octant in range(8):
        own_x, own_y, own_z = (octant % 2, octant // 2 % 2, octant // 4)
        column = 0
        for parent_x in (-1, 0, 1):
            for parent_y in (-1, 0, 1):
                for parent_z in (-1, 0, 1):
                    for child in range(8):
                        step_x = 2 * parent_x + child % 2 - own_x
                        step_y = 2 * parent_y + child // 2 % 2 - own_y
                        step_z = 2 * parent_z + child // 4 - own_z
                        if max(abs(step_x), abs(step_y), abs(step_z)) > 1:
                            result[octant, column] = far_offsets[step_x, step_y, step_z]
                            column = column + 1
    return result


def entry_to_lane():
    table = direction_table()
    result = np.zeros((8, 189, 512), np.float32)
    for octant in range(8):
        for entry in range(189):
            row, half = divmod(int(table[octant, entry]), 2)
            if row < 128:
                result[octant, entry, 128 * half + row] = 1
            else:
                for copy in range(4):
                    result[octant, entry, 256 + 128 * half + 32 * copy + row - 128] = 1
    return result.astype(ml_dtypes.bfloat16)


K = 136
LB = 17
MAIN = LB * 128
DEPTH = MAIN + 640
ROWS = 158
WIDE = 17 * 128
BF16 = jnp.bfloat16
F32 = jnp.float32


def translate_kernel(
    jumps, src_f, src_c, fine_lists, fine_flags, coarse_lists, coarse_flags, perm, trans,
    out_f, out_c, idx, v, g0, g1, r,
):
    step = pl.program_id(0)
    cells = out_f.shape[0]
    coarse_cells = out_c.shape[0]

    @pl.when(step == 0)
    def _():
        places = coarse_lists[...]
        moved = places
        for start, gap in jumps:
            moved = moved + jnp.where(places >= start, gap, 0)
        fine = jnp.where(fine_flags[...] == 1, fine_lists[...] + 1, 0)
        coarse = jnp.where(coarse_flags[...] == 1, moved + 1, 0)
        total = cells + coarse_cells
        both = jnp.concatenate([fine, coarse], axis=0)
        digits = jnp.concatenate([both >> 6, both & 63], axis=0).astype(F32).astype(BF16)
        octant = lax.broadcasted_iota(jnp.int32, (total, 512), 0) % 8
        found = jnp.zeros((total, 512), F32)
        for o in range(8):
            x = jnp.dot(digits, perm[o], preferred_element_type=F32)
            found = jnp.where(octant == o, x[:total] * 64.0 + x[total:], found)
        idx[...] = found.astype(jnp.int32) - 1
        v[MAIN + LB * 32 :, :] = jnp.zeros((DEPTH - MAIN - LB * 32, WIDE), BF16)

    first = jnp.where(step < 8, 16 * step, MAIN + 16 * (step - 8))
    stride = jnp.where(step < 8, 128, 32)
    lane = lax.broadcasted_iota(jnp.int32, (16, 128), 1)
    live = (lax.broadcasted_iota(jnp.int32, (16, 128), 0) + 16 * step) < ROWS
    bits = [(lane // (8 << b)) % 2 == 1 for b in range(4)]

    def group(g, last=False):
        base = g * WIDE
        d = [trans[:, base + 128 * j : base + 128 * j + 128] for j in range(17)]
        if last:
            d = [jnp.where(live, x, 0.0) for x in d]
        for b in range(4):
            d = [jnp.where(bits[b], d[(m + (1 << b)) % 17], d[m]) for m in range(17)]
        for lb in range(17):
            piece = d[-lb % 17]
            turn = (-8 * lb) % 128
            if turn:
                piece = pltpu.roll(piece, turn, 1)
            row = pl.multiple_of(first + lb * stride, 16)
            v[pl.ds(row, 16), 128 * g : 128 * g + 128] = piece


    quarter = lax.broadcasted_iota(jnp.int32, (16, 128), 1) // 32

    def fetch_pair(src, low_row, high_row, out_row):
        places = lax.broadcasted_iota(jnp.int32, (src.shape[1], 512), 0).astype(jnp.int16)
        both = []
        for place in (low_row, high_row):
            wanted = jnp.broadcast_to(idx[pl.ds(place, 1), :], (16, 512)).astype(jnp.int16)
            wanted = jnp.broadcast_to(wanted[None], (src.shape[1] // 16, 16, 512))
            hot = jnp.where(
                places == wanted.reshape(src.shape[1], 512), jnp.ones((), BF16), jnp.zeros((), BF16)
            )
            both.append(jnp.dot(src[...], hot, preferred_element_type=F32))
        tiles = [
            jnp.concatenate([x[8 * lb : 8 * lb + 8] for x in both], axis=0) for lb in range(LB)
        ]
        rows = pl.ds(pl.multiple_of(out_row, 16), 16)
        for half, g in ((0, g0), (1, g1)):
            for lb in range(LB):
                g[rows, 128 * lb : 128 * lb + 128] = tiles[lb][:, 128 * half : 128 * half + 128].astype(BF16)
            for m in range(5):
                total = jnp.zeros((16, 128), F32)
                for j in range(4):
                    if 4 * m + j < LB:
                        part = tiles[4 * m + j][:, 256 + 128 * half : 384 + 128 * half]
                        total = jnp.where(quarter == j, part, total)
                g[rows, MAIN + 128 * m : MAIN + 128 * m + 128] = total.astype(BF16)

    @pl.when(step < 8)
    def _():
        for g in range(17):
            group(g)
        for i in range(4):
            fetch_pair(src_f, 8 * step + 2 * i, 8 * step + 2 * i + 1, 64 * step + 16 * i)

    @pl.when(step == 8)
    def _():
        for g in range(17):
            group(g)
        for i in range(coarse_cells // 2):
            fetch_pair(src_c, cells + 2 * i, cells + 2 * i + 1, 8 * cells + 16 * i)

    @pl.when(step == 9)
    def _():
        for g in range(17):
            group(g, last=True)

        def product(g, from_column, to_column, width):
            x = jnp.dot(g[...], v[:, pl.ds(from_column, width)], preferred_element_type=F32)
            same = (
                lax.broadcasted_iota(jnp.int32, x.shape, 0) % 8
                == lax.broadcasted_iota(jnp.int32, x.shape, 1) % 8
            )
            x = jnp.where(same, x, 0.0).reshape(x.shape[0] // 8, 8, width).sum(axis=1)
            r[:, pl.ds(to_column, width)] = x

        for n in range(4):
            product(g0, 256 * n, 256 * n, 256)
            product(g1, 1152 + 256 * n, 1280 + 256 * n, 256)
        product(g0, 1024, 1024, 128)
        product(g1, 1024, 1152, 128)
        column = lax.broadcasted_iota(jnp.int32, (K, 2304), 1)
        k = jnp.where(column < 1152, column // 8, (column - 128) // 8 - K)
        hit = jnp.where(k == lax.broadcasted_iota(jnp.int32, (K, 2304), 0), 1.0, 0.0).astype(BF16)
        out = jnp.zeros((cells + coarse_cells, K), F32)
        rest = r[...]
        for _ in range(3):
            piece = rest.astype(BF16)
            rest = rest - piece.astype(F32)
            out = out + lax.dot_general(
                piece, hit, (((1,), (1,)), ((), ())), preferred_element_type=F32
            )
        out_f[...] = out[:cells]
        out_c[...] = out[cells:]


def translate(jumps, src_f, src_c, lists, perm, translators):
    cells, coarse_cells = lists[0].shape[0], lists[2].shape[0]
    total = cells + coarse_cells

    def whole(x):
        return pl.BlockSpec(x.shape, lambda s: (0,) * x.ndim)

    return pl.pallas_call(
        functools.partial(translate_kernel, jumps),
        grid=(10,),
        in_specs=[
            whole(src_f), whole(src_c), *[whole(x) for x in lists], whole(perm),
            pl.BlockSpec((16, translators.shape[1]), lambda s: (s, 0)),
        ],
        out_specs=[
            pl.BlockSpec((cells, K), lambda s: (0, 0)),
            pl.BlockSpec((coarse_cells, K), lambda s: (0, 0)),
        ],
        out_shape=[
            jax.ShapeDtypeStruct((cells, K), F32),
            jax.ShapeDtypeStruct((coarse_cells, K), F32),
        ],
        scratch_shapes=[
            pltpu.VMEM((total, 512), jnp.int32),
            pltpu.VMEM((DEPTH, WIDE), BF16),
            pltpu.VMEM((8 * total, DEPTH), BF16),
            pltpu.VMEM((8 * total, DEPTH), BF16),
            pltpu.VMEM((total, 2304), F32),
        ],
        compiler_params=pltpu.CompilerParams(vmem_limit_bytes=56 * 2**20),
    )(src_f, src_c, *lists, perm, translators)


def round_up(count):
    return -(-count // 16) * 16


def exchange_kernel(
    n_gx, n_gy, plan, exp_f, side_f, sel_c, mult, out_f, out_c, picked, buf_f, buf_c, send_sems, recv_sems
):
    i = lax.axis_index("gx")
    j = lax.axis_index("gy")
    mesh_ids = pl.DeviceIdType.MESH
    barrier = pltpu.get_barrier_semaphore()
    for d in range(1, n_gy):
        peer = lax.rem(j + d, n_gy)
        pl.semaphore_signal(barrier, inc=1, device_id=(i, peer), device_id_type=mesh_ids)

    @pl.when(i > 0)
    def _():
        pl.semaphore_signal(barrier, inc=1, device_id=(i - 1, j), device_id_type=mesh_ids)

    @pl.when(i < n_gx - 1)
    def _():
        pl.semaphore_signal(barrier, inc=1, device_id=(i + 1, j), device_id_type=mesh_ids)

    own = plan[0][0]
    depth = mult.shape[0]
    wanted = [lax.broadcasted_iota(jnp.int32, (1, own), 1)]
    wanted += [exp_f[0, p : p + 1, :] for p in range(n_gy)]
    wanted += [side_f[0, t : t + 1, :] for t in range(2)]
    wanted += [sel_c[p : p + 1, :] for p in range(sel_c.shape[0])]
    wanted = jnp.concatenate(wanted, axis=1)
    hot = jnp.where(
        wanted == lax.broadcasted_iota(jnp.int32, (depth, wanted.shape[1]), 0), 1.0, 0.0
    )
    picked[...] = jnp.dot(hot.T.astype(BF16), mult[...], preferred_element_type=F32).astype(BF16)
    pl.semaphore_wait(barrier, n_gy - 1 + jnp.where(i > 0, 1, 0) + jnp.where(i < n_gx - 1, 1, 0))

    def row(start):
        return pl.multiple_of(start, 16)

    copies = []
    for level, (buf, own, cap, side, base) in enumerate(zip((buf_f, buf_c), *plan)):
        for d in range(1, n_gy):
            peer = lax.rem(j + d, n_gy)
            copy = pltpu.make_async_remote_copy(
                src_ref=picked.at[pl.ds(row(base + own + cap * peer), cap)],
                dst_ref=buf.at[pl.ds(row(own + cap * j), cap)],
                send_sem=send_sems.at[level, d],
                recv_sem=recv_sems.at[level, d],
                device_id=(i, peer),
                device_id_type=mesh_ids,
            )
            copy.start()
            copies.append(copy)
    neighbours = []
    for level, (buf, own, cap, side, base) in enumerate(zip((buf_f, buf_c), *plan)):
        first = own + cap * n_gy
        for turn, there in ((0, i + 1), (1, i - 1)):
            copy = pltpu.make_async_remote_copy(
                src_ref=picked.at[pl.ds(base + first + side * turn, side)],
                dst_ref=buf.at[pl.ds(first + side * turn, side)],
                send_sem=send_sems.at[level, n_gy + turn],
                recv_sem=recv_sems.at[level, n_gy + turn],
                device_id=(there, j),
                device_id_type=mesh_ids,
            )
            sends = (i < n_gx - 1) if turn == 0 else (i > 0)
            receives = (i > 0) if turn == 0 else (i < n_gx - 1)
            neighbours.append((copy, sends, receives))
            pl.when(sends)(copy.start)

            @pl.when(jnp.logical_not(receives))
            def _(buf=buf, start=first + side * turn, side=side):
                buf[pl.ds(start, side), :] = jnp.zeros((side, K), BF16)

        buf[:own, :] = picked[base : base + own, :]
        buf[pl.ds(row(own + cap * j), cap), :] = picked[pl.ds(row(base + own + cap * j), cap), :]
    for copy in copies:
        copy.wait_send()
        copy.wait_recv()
    for copy, sends, receives in neighbours:
        pl.when(sends)(copy.wait_send)
        pl.when(receives)(copy.wait_recv)
    out_f[...] = buf_f[...].T
    out_c[...] = buf_c[...].T


def exchange(mult, coarse, fine_exports, fine_sides, coarse_exports, coarse_sides):
    n_gx, n_gy = lax.axis_size("gx"), lax.axis_size("gy")
    own_f, own_c = mult.shape[0], coarse.shape[0]

    parts = [jnp.arange(own_c, dtype=jnp.int32)[None], coarse_exports[0], coarse_sides[0]]
    sel_c = jnp.concatenate(
        [
            jnp.pad(p + own_f, ((0, 0), (0, round_up(p.shape[1]) - p.shape[1])), constant_values=-1)
            for p in parts
        ]
    )
    rows_f = own_f + fine_exports[0].size + fine_sides[0].size
    rows_c = sel_c.size
    both = jnp.concatenate([mult, coarse], axis=0)
    plan = (
        (round_up(own_f), round_up(own_c)),
        (round_up(fine_exports.shape[2]), round_up(coarse_exports.shape[2])),
        (round_up(fine_sides.shape[2]), round_up(coarse_sides.shape[2])),
        (0, rows_f),
    )
    vmem = pl.BlockSpec(memory_space=pltpu.VMEM)
    return pl.pallas_call(
        functools.partial(exchange_kernel, n_gx, n_gy, plan),
        in_specs=[vmem] * 4,
        out_specs=[vmem, vmem],
        out_shape=[
            jax.ShapeDtypeStruct((K, rows_f), BF16),
            jax.ShapeDtypeStruct((K, rows_c), BF16),
        ],
        scratch_shapes=[
            pltpu.VMEM((rows_f + rows_c, K), BF16),
            pltpu.VMEM((rows_f, K), BF16),
            pltpu.VMEM((rows_c, K), BF16),
            pltpu.SemaphoreType.DMA((2, n_gy + 2)),
            pltpu.SemaphoreType.DMA((2, n_gy + 2)),
        ],
        compiler_params=pltpu.CompilerParams(
            collective_id=0, has_side_effects=True, vmem_limit_bytes=32 * 2**20
        ),
    )(fine_exports, fine_sides, sel_c, both)


def shards(
    multipoles,
    parent_ops,
    translators,
    fine_exports,
    fine_sides,
    fine_lists,
    fine_flags,
    coarse_exports,
    coarse_sides,
    coarse_lists,
    coarse_flags,
):
    coeffs = multipoles.shape[0]
    octant_ops = parent_ops.reshape(8, coeffs, coeffs)
    children = multipoles.T.reshape(-1, 8, coeffs)
    coarse = jnp.einsum(
        "okl,qol->qk", octant_ops, children, preferred_element_type=jnp.float32
    ).astype(jnp.bfloat16)
    fine_buffer, coarse_buffer = exchange(
        multipoles.T, coarse, fine_exports, fine_sides, coarse_exports, coarse_sides
    )
    own = coarse.shape[0]
    peers, cap = coarse_exports.shape[1:]
    side = coarse_sides.shape[2]
    jumps = [(own, round_up(own) - own)]
    jumps += [(own + cap * p, round_up(cap) - cap) for p in range(1, peers + 1)]
    jumps += [(own + cap * peers + side, round_up(side) - side)]
    lists = [x.T for x in (fine_lists, fine_flags, coarse_lists, coarse_flags)]
    perm = jnp.asarray(entry_to_lane())
    fine, coarse = translate(jumps, fine_buffer, coarse_buffer, lists, perm, translators)
    return fine.T, coarse.T


def solution(mesh):
    return jax.shard_map(
        shards,
        mesh=mesh,
        in_specs=(
            P(None, ("gx", "gy")),
            P(),
            P(),
            P(("gx", "gy"), None, None),
            P(("gx", "gy"), None, None),
            P(None, ("gx", "gy")),
            P(None, ("gx", "gy")),
            P(("gx", "gy"), None, None),
            P(("gx", "gy"), None, None),
            P(None, ("gx", "gy")),
            P(None, ("gx", "gy")),
        ),
        out_specs=(P(None, ("gx", "gy")), P(None, ("gx", "gy"))),
        check_vma=False,
    )
```
